512 devices in a mesh: fsdp: 64 (over z, x), tensor: 8 (over y, core).
Axes of the slice: x: 4, y: 4, z: 16, core: 2. Of those that a mesh axis runs over, the one named last changes fastest.
Arguments:
- momentum: float32 [8192, 28672], P('fsdp', 'tensor'), may hold values from -405 to 405
- gradient: bfloat16 [8192, 28672], P('fsdp', 'tensor'), may hold values from -6 to 6
- basis: float32 [28672, 256], P('tensor', 'fsdp'), may hold values from -0.03125 to 0.03125
Outputs:
- new_momentum: float32 [8192, 28672], P('fsdp', 'tensor')
- orthonormal: float32 [8192, 256], P('fsdp')
- new_basis: float32 [28672, 256], P('tensor', 'fsdp')
The draws below stay inside these ranges and needn't reach their ends.
All inputs are finite; a program needn't handle non-finite values.
Results may differ from the reference program's by a relative error of at most 0.0003.
Values sent between devices are 32-bit elements; how exact they have to be, the bound alone decides.
No kernel may reach another device: no remote copies, remote signals or barrier semaphores. Data moves between devices by JAX's collectives and lax.ppermute only.
A program may use at most 64 MiB of HBM per device.

```python
import jax
import jax.numpy as jnp
from jax import lax

D = 8192
FF = 28672
RANK = 256


def draw_momentum(key, part):
    key = jax.random.fold_in(key, 11)
    key_base = jax.random.fold_in(key, 1)
    key_rough = jax.random.fold_in(key, 2)
    key_column = jax.random.fold_in(key, 3)
    position = jnp.arange(D, dtype=jnp.float32) / D
    column_pos = jnp.arange(FF, dtype=jnp.float32) / FF
    base = jnp.clip(jax.random.normal(key_base, (D, FF), jnp.float32), -6.0, 6.0)
    profile = 10.0 ** (2.0 * position - 1.0)
    column_profile = 10.0 ** (0.7 * (column_pos - 0.5))
    rough = jnp.exp(jax.random.uniform(key_rough, (D,), jnp.float32, 0.0, 1.0986))
    column_rough = jnp.exp(jax.random.uniform(key_column, (FF,), jnp.float32, 0.0, 1.0986)) / 1.82
    return (base * (profile * rough)[:, None] * (column_profile * column_rough)[None, :]).astype(jnp.float32)


def shard_levels(key, dims, split, least, high):
    level, own = 1.0, jax.random.fold_in(key, 6)
    for axis_at, blocks in split:
        steps = jnp.exp(jax.random.uniform(jax.random.fold_in(own, axis_at), (blocks,), jnp.float32, least / len(split), high / len(split)))
        level = level * jnp.repeat(steps, dims[axis_at] // blocks).reshape([-1 if axis == axis_at else 1 for axis in range(len(dims))])
    return level


def normal_values(key, extent, width, reach, split=(), held_as=jnp.bfloat16):
    factor_of = shard_levels(key, extent, split, -0.22, 0.18) if split else 1.0
    entries = jax.random.normal(key, extent, jnp.float32) * width * factor_of
    return jnp.minimum(jnp.maximum(entries, -reach), reach).astype(held_as)


def setup_inputs(seed: int = 0) -> dict:
    key_of = jax.random.split(jax.random.key(seed), 4)
    return {
        "momentum": draw_momentum(jax.random.fold_in(key_of[3], 71), 0),
        "gradient": normal_values(key_of[1], (D, FF), 1.0, 6.0, ((0, 64), (1, 8))),
        "basis": normal_values(key_of[2], (FF, RANK), FF ** -0.5, 0.03125, ((0, 8), (1, 64)), jnp.float32),
    }


momentum_keep = 0.95
column_eps = 1e-08

def reference(momentum, gradient, basis):
    high = lax.Precision.HIGHEST
    buffer = momentum + gradient.astype(jnp.float32)
    left_raw = jnp.dot(buffer.astype(jnp.float32), basis.astype(jnp.float32), precision=high, preferred_element_type=jnp.float32)
    gram_matrix = lax.dot_general(left_raw.astype(jnp.float32), left_raw.astype(jnp.float32), (((0,), (0,)), ((), ())), precision=high, preferred_element_type=jnp.float32)
    factor = jnp.linalg.cholesky(gram_matrix)
    orthonormal = jax.scipy.linalg.solve_triangular(factor, left_raw.T, lower=True).T
    right_raw = lax.dot_general(buffer.astype(jnp.float32), orthonormal.astype(jnp.float32), (((0,), (0,)), ((), ())), precision=high, preferred_element_type=jnp.float32)
    feedback = lax.dot_general(orthonormal.astype(jnp.float32), right_raw.astype(jnp.float32), (((1,), (1,)), ((), ())), precision=high, preferred_element_type=jnp.float32)
    new_momentum = buffer - (1.0 - momentum_keep) * feedback
    norm_values = jnp.sqrt(lax.optimization_barrier(jnp.sum(right_raw * right_raw, axis=0))) + column_eps
    new_basis = right_raw / norm_values
    return (new_momentum, orthonormal, new_basis)
```

```python
import jax
import jax.numpy as jnp
from jax import lax
from jax.experimental import pallas as pl
from jax.experimental.pallas import tpu as pltpu
from jax.sharding import Mesh
from jax.sharding import PartitionSpec as P

momentum_keep = 0.95
column_eps = 1e-08
high = lax.Precision.HIGHEST

Z = ("zh", "zl")
GROUP = ("x", "y", "core")
HALF = 128


def dot(a, b, contract, precision=high):
    return lax.dot_general(
        a, b, ((contract[:1], contract[1:]), ((), ())), precision=precision, preferred_element_type=jnp.float32
    )


def inverse_factor_block(block):
    n = block.shape[0]
    groups = [block[8 * g : 8 * g + 8, :] for g in range(n // 8)]
    lane = lax.broadcasted_iota(jnp.int32, (1, n), 1)
    row_in_group = lax.broadcasted_iota(jnp.int32, (8, n), 0)
    for k in range(0, n, 4):
        first, at = k // 8, k % 8
        inside = (lane >= k) & (lane < k + 4)
        cols = {
            g: [jnp.broadcast_to(groups[g][:, k + j : k + j + 1], (8, n)) for j in range(4)]
            for g in range(first, n // 8)
        }
        a = [[cols[first][j][at + i : at + i + 1, :] for j in range(i + 1)] for i in range(4)]
        low = [[None] * 4 for _ in range(4)]
        inv = [[None] * 4 for _ in range(4)]
        for j in range(4):
            pivot = a[j][j]
            for m in range(j):
                pivot = pivot - low[j][m] * low[j][m]
            r = lax.rsqrt(pivot)
            r = r * (1.5 - 0.5 * (pivot * r) * r)
            inv[j][j] = r
            for i in range(j + 1, 4):
                value = a[i][j]
                for m in range(j):
                    value = value - low[i][m] * low[j][m]
                low[i][j] = value * r
        for j in range(4):
            for i in range(j + 1, 4):
                value = low[i][j] * inv[j][j]
                for m in range(j + 1, i):
                    value = value + low[i][m] * inv[m][j]
                inv[i][j] = -(value * inv[i][i])
        rows = []
        for i in range(4):
            unit = jnp.where(lane == k + i, 1.0, 0.0)
            rows.append(jnp.where(inside, unit, groups[first][at + i : at + i + 1, :]))
        new = []
        for j in range(4):
            value = inv[j][0] * rows[0]
            for i in range(1, j + 1):
                value = value + inv[j][i] * rows[i]
            new.append(value)
        for g in range(first, n // 8):
            if g == first and at == 4:
                updated = groups[g]
            else:
                updated = jnp.where(inside, 0.0, groups[g])
                for j in range(4):
                    factor = inv[j][0] * cols[g][0]
                    for i in range(1, j + 1):
                        factor = factor + inv[j][i] * cols[g][i]
                    updated = updated - factor * new[j]
            if g == first:
                if at == 4:
                    updated = groups[g]
                for j in range(4):
                    updated = jnp.where(row_in_group == at + j, new[j], updated)
            groups[g] = updated
    whole = jnp.concatenate(groups, axis=0)
    rows_at = lax.broadcasted_iota(jnp.int32, (n, n), 0)
    cols_at = lax.broadcasted_iota(jnp.int32, (n, n), 1)
    return jnp.where(rows_at >= cols_at, whole, 0.0)


def inverse_factor_kernel(gram_ref, out_ref):
    top = slice(0, HALF)
    low = slice(HALF, 2 * HALF)
    x11 = inverse_factor_block(gram_ref[top, top])
    u = dot(x11, gram_ref[top, low], (1, 0))
    rest = gram_ref[low, low] - dot(u, u, (0, 0))
    t = dot(u, x11, (0, 0))
    x22 = inverse_factor_block(rest)
    out_ref[top, top] = x11
    out_ref[top, low] = jnp.zeros((HALF, HALF), jnp.float32)
    out_ref[low, top] = -dot(x22, t, (1, 0))
    out_ref[low, low] = x22


def inverse_factor(gram):
    vmem = pl.BlockSpec(memory_space=pltpu.VMEM)
    return pl.pallas_call(
        inverse_factor_kernel,
        out_shape=jax.ShapeDtypeStruct(gram.shape, jnp.float32),
        in_specs=[vmem],
        out_specs=vmem,
        compiler_params=pltpu.CompilerParams(vmem_limit_bytes=16 << 20),
        cost_estimate=pl.CostEstimate(flops=2 * 256**3, bytes_accessed=2 * 256 * 256 * 4, transcendentals=256),
    )(gram)


def on_device(momentum, gradient, basis):
    rows, columns = momentum.shape
    ranks = basis.shape[1]
    rank = 256
    nx, ny = lax.axis_size("x"), lax.axis_size("y")
    nzh, nzl = lax.axis_size("zh"), lax.axis_size("zl")
    nz = nzh * nzl
    part = columns // nx
    x_at, y_at = lax.axis_index("x"), lax.axis_index("y")

    buffer = momentum + gradient.astype(jnp.float32)
    tall = lax.all_to_all(buffer.reshape(rows, nx, part).transpose(1, 0, 2), "x", 0, 0, tiled=True)
    tall = tall.reshape(nx * rows, part)
    v = lax.all_to_all(basis.T.reshape(ranks, nx, part).transpose(1, 0, 2), "x", 0, 0, tiled=True)
    v = lax.all_gather(v.reshape(nx * ranks, part), Z, axis=0, tiled=True)

    partial = dot(tall, v, (1, 1))
    peers = lax.axis_size(GROUP)
    piece = partial.shape[0] // peers
    parts = lax.all_to_all(partial.reshape(peers, piece, rank), GROUP, 0, 0, tiled=True)
    own = jnp.sum(parts, axis=0)
    left = lax.all_to_all(jnp.broadcast_to(own[None], (peers, piece, rank)), GROUP, 0, 0, tiled=True)
    left = left.reshape(nx * rows, rank)

    slab = rank // ny
    w_part = dot(left, tall, (0, 0))
    g_part = dot(left, lax.dynamic_slice_in_dim(left, y_at * slab, slab, 1), (0, 0))
    both = jnp.concatenate([w_part, g_part], axis=1).reshape(nzh, nzl, rank // nz, part + slab)
    both = jnp.sum(lax.all_to_all(both, "zl", 1, 1, tiled=True), axis=1)
    both = jnp.sum(lax.all_to_all(both, "zh", 0, 0, tiled=True), axis=0)
    both = lax.all_gather(both, Z, axis=0, tiled=True)
    w = both[:, :part]
    gram = lax.all_gather(both[:, part:].T, "y", axis=0, tiled=True)
    inverse = inverse_factor((gram + gram.T) * 0.5)

    ortho = dot(left, inverse, (1, 1))
    orthonormal = lax.dynamic_slice_in_dim(ortho, x_at * rows, rows, 0)
    right = dot(inverse, w, (1, 0))

    z_at = lax.axis_index(Z)
    mine = lax.dynamic_slice_in_dim(right, z_at * (nx * ranks), nx * ranks, 0)
    mine = lax.all_to_all(mine.reshape(nx, ranks, part), "x", 0, 0, tiled=True)
    mine = mine.transpose(1, 0, 2).reshape(ranks, columns)
    squares = lax.psum(jnp.sum(mine * mine, axis=1), ("y", "core"))
    new_basis = (mine / (jnp.sqrt(squares) + column_eps)[:, None]).T

    feedback = dot(ortho, right, (1, 0))
    feedback = lax.all_to_all(feedback.reshape(nx, rows, part), "x", 0, 0, tiled=True)
    feedback = feedback.transpose(1, 0, 2).reshape(rows, columns)
    new_momentum = buffer - (1.0 - momentum_keep) * feedback
    return (new_momentum, orthonormal, new_basis)


def solution(mesh):
    fine = Mesh(mesh.devices.reshape(4, 4, 4, 4, 2), ("zh", "zl", "x", "y", "core"))
    fsdp, tensor = ("zh", "zl", "x"), ("y", "core")
    return jax.shard_map(
        on_device,
        mesh=fine,
        in_specs=(P(fsdp, tensor), P(fsdp, tensor), P(tensor, fsdp)),
        out_specs=(P(fsdp, tensor), P(fsdp, None), P(tensor, fsdp)),
        check_vma=False,
    )
```

```python
import functools

import jax
import jax.numpy as jnp
from jax import lax
from jax.experimental import pallas as pl
from jax.experimental.pallas import tpu as pltpu
from jax.sharding import Mesh
from jax.sharding import PartitionSpec as P

momentum_keep = 0.95
column_eps = 1e-08
high = lax.Precision.HIGHEST

Z = ("zh", "zl")
GROUP = ("x", "y", "core")
HALF = 128
LANES = 128


def dot(a, b, contract, precision=high):
    return lax.dot_general(
        a, b, ((contract[:1], contract[1:]), ((), ())), precision=precision, preferred_element_type=jnp.float32
    )


def inverse_factor_block(block):
    n = block.shape[0]
    groups = [block[8 * g : 8 * g + 8, :] for g in range(n // 8)]
    lane = lax.broadcasted_iota(jnp.int32, (1, n), 1)
    row_in_group = lax.broadcasted_iota(jnp.int32, (8, n), 0)
    for k in range(0, n, 4):
        first, at = k // 8, k % 8
        inside = (lane >= k) & (lane < k + 4)
        cols = {
            g: [jnp.broadcast_to(groups[g][:, k + j : k + j + 1], (8, n)) for j in range(4)]
            for g in range(first, n // 8)
        }
        a = [[cols[first][j][at + i : at + i + 1, :] for j in range(i + 1)] for i in range(4)]
        low = [[None] * 4 for _ in range(4)]
        inv = [[None] * 4 for _ in range(4)]
        for j in range(4):
            pivot = a[j][j]
            for m in range(j):
                pivot = pivot - low[j][m] * low[j][m]
            r = lax.rsqrt(pivot)
            inv[j][j] = r
            for i in range(j + 1, 4):
                value = a[i][j]
                for m in range(j):
                    value = value - low[i][m] * low[j][m]
                low[i][j] = value * r
        for j in range(4):
            for i in range(j + 1, 4):
                value = low[i][j] * inv[j][j]
                for m in range(j + 1, i):
                    value = value + low[i][m] * inv[m][j]
                inv[i][j] = -(value * inv[i][i])
        rows = []
        for i in range(4):
            unit = jnp.where(lane == k + i, 1.0, 0.0)
            rows.append(jnp.where(inside, unit, groups[first][at + i : at + i + 1, :]))
        new = []
        for j in range(4):
            value = inv[j][0] * rows[0]
            for i in range(1, j + 1):
                value = value + inv[j][i] * rows[i]
            new.append(value)
        for g in range(first, n // 8):
            if g == first and at == 4:
                updated = groups[g]
            else:
                updated = jnp.where(inside, 0.0, groups[g])
                for j in range(4):
                    factor = inv[j][0] * cols[g][0]
                    for i in range(1, j + 1):
                        factor = factor + inv[j][i] * cols[g][i]
                    updated = updated - factor * new[j]
            if g == first:
                if at == 4:
                    updated = groups[g]
                for j in range(4):
                    updated = jnp.where(row_in_group == at + j, new[j], updated)
            groups[g] = updated
    whole = jnp.concatenate(groups, axis=0)
    rows_at = lax.broadcasted_iota(jnp.int32, (n, n), 0)
    cols_at = lax.broadcasted_iota(jnp.int32, (n, n), 1)
    return jnp.where(rows_at >= cols_at, whole, 0.0)


def inverse_factor(gram):
    x11 = inverse_factor_block(gram[:HALF, :HALF])
    u = dot(x11, gram[:HALF, HALF:], (1, 0))
    rest = gram[HALF:, HALF:] - dot(u, u, (0, 0))
    t = dot(u, x11, (0, 0))
    x22 = inverse_factor_block(rest)
    return x11, -dot(x22, t, (1, 0)), x22


def split_kernel(momentum_ref, gradient_ref, out_ref):
    out_ref[0] = momentum_ref[...] + gradient_ref[...].astype(jnp.float32)


def split(momentum, gradient, parts):
    rows, columns = momentum.shape
    part = columns // parts
    block = pl.BlockSpec((rows, part), lambda i: (0, i))
    return pl.pallas_call(
        split_kernel,
        grid=(parts,),
        out_shape=jax.ShapeDtypeStruct((parts, rows, part), jnp.float32),
        in_specs=[block, block],
        out_specs=pl.BlockSpec((1, rows, part), lambda i: (i, 0, 0)),
        compiler_params=pltpu.CompilerParams(vmem_limit_bytes=16 << 20),
        cost_estimate=pl.CostEstimate(flops=momentum.size, bytes_accessed=10 * momentum.size, transcendentals=0),
    )(momentum, gradient)


def join_kernel(buffer_ref, back_ref, squares_ref, momentum_ref, basis_ref):
    rows = momentum_ref.shape[0]
    momentum_ref[...] = buffer_ref[0] - (1.0 - momentum_keep) * back_ref[0, :rows, :]
    basis_ref[...] = back_ref[0, rows:, :] / (jnp.sqrt(squares_ref[...]) + column_eps)


def join(buffer, back, squares):
    parts, rows, part = buffer.shape
    ranks = back.shape[1] - rows
    return pl.pallas_call(
        join_kernel,
        grid=(parts,),
        out_shape=(
            jax.ShapeDtypeStruct((rows, parts * part), jnp.float32),
            jax.ShapeDtypeStruct((ranks, parts * part), jnp.float32),
        ),
        in_specs=[
            pl.BlockSpec((1, rows, part), lambda i: (i, 0, 0)),
            pl.BlockSpec((1, rows + ranks, part), lambda i: (i, 0, 0)),
            pl.BlockSpec((ranks, 1), lambda i: (0, 0)),
        ],
        out_specs=(pl.BlockSpec((rows, part), lambda i: (0, i)), pl.BlockSpec((ranks, part), lambda i: (0, i))),
        compiler_params=pltpu.CompilerParams(vmem_limit_bytes=16 << 20),
        cost_estimate=pl.CostEstimate(flops=2 * buffer.size, bytes_accessed=12 * buffer.size, transcendentals=0),
    )(buffer, back, squares)


def sums_kernel(nzh, nzl, left_ref, tall_ref, out_ref, gram_ref):
    y_at = lax.axis_index("y")
    ranks = left_ref.shape[1] // (nzh * nzl)
    tiles = tall_ref.shape[1] // LANES
    left = left_ref[...]
    gram_ref[...] = dot(left, left, (0, 0))
    w = dot(left, tall_ref[...], (0, 0))
    half = ranks // 2
    lanes = pl.ds(pl.multiple_of((y_at % 2) * LANES, LANES), LANES)
    for zh in range(nzh):
        for zl in range(nzl):
            first = (zh * nzl + zl) * ranks
            for t in range(tiles):
                out_ref[zl * nzh + zh, t * ranks : (t + 1) * ranks, :] = w[
                    first : first + ranks, t * LANES : (t + 1) * LANES
                ]
            piece = pl.ds(pl.multiple_of(first + (y_at // 2) * half, half), half)
            out_ref[zl * nzh + zh, tiles * ranks :, :] = gram_ref[piece, lanes]


def sums(left, tall, nzh, nzl):
    rank, part = left.shape[1], tall.shape[1]
    ranks = rank // (nzh * nzl)
    rows = part // LANES * ranks + ranks // 2
    vmem = pl.BlockSpec(memory_space=pltpu.VMEM)
    return pl.pallas_call(
        functools.partial(sums_kernel, nzh, nzl),
        out_shape=jax.ShapeDtypeStruct((nzl * nzh, rows, LANES), jnp.float32),
        in_specs=[vmem, vmem],
        out_specs=vmem,
        scratch_shapes=[pltpu.VMEM((rank, rank), jnp.float32)],
        compiler_params=pltpu.CompilerParams(vmem_limit_bytes=24 << 20),
        cost_estimate=pl.CostEstimate(
            flops=12 * left.shape[0] * rank * (part + rank), bytes_accessed=4 * left.size + 8 * tall.size, transcendentals=0
        ),
    )(left, tall)


def finish_kernel(nx, gram_ref, left_ref, w_ref, back_ref, ortho_ref, squares_ref, inverse_ref, all_ref, right_ref):
    x_at, z_at = lax.axis_index("x"), lax.axis_index(Z)
    nz, slab, _ = w_ref.shape
    rank = inverse_ref.shape[0]
    ranks = rank // nz
    rows = left_ref.shape[0] // nx
    half = ranks // 2
    x11, x21, x22 = inverse_factor(gram_ref[...])
    inverse_ref[:HALF, :HALF] = x11
    inverse_ref[:HALF, HALF:] = jnp.zeros((HALF, HALF), jnp.float32)
    inverse_ref[HALF:, :HALF] = x21
    inverse_ref[HALF:, HALF:] = x22
    inverse = inverse_ref[...]
    tiles = (slab - half) // ranks
    for t in range(tiles):
        w = jnp.concatenate([w_ref[z, t * ranks : (t + 1) * ranks, :] for z in range(nz)], axis=0)
        right_ref[:, t * LANES : (t + 1) * LANES] = dot(inverse, w, (1, 0))
    all_ref[...] = dot(left_ref[...], inverse, (1, 1))
    ortho_ref[...] = all_ref[pl.ds(pl.multiple_of(x_at * rows, rows), rows), :]

    right = right_ref[...]
    right_high = right.astype(jnp.bfloat16)
    right_low = (right - right_high.astype(jnp.float32)).astype(jnp.bfloat16)
    for x in range(nx):
        q = all_ref[x * rows : (x + 1) * rows, :]
        q_high = q.astype(jnp.bfloat16)
        q_low = (q - q_high.astype(jnp.float32)).astype(jnp.bfloat16)
        plain = lax.Precision.DEFAULT
        small = dot(q_low, right_high, (1, 0), plain) + dot(q_high, right_low, (1, 0), plain)
        back_ref[x, :rows, :] = small + dot(q_high, right_high, (1, 0), plain)
    mine = right_ref[pl.ds(pl.multiple_of(z_at * ranks, ranks), ranks), :]
    each = ranks // nx
    for x in range(nx):
        back_ref[x, rows : rows + each, :] = mine[x * each : (x + 1) * each, :]
    squares_ref[...] = jnp.broadcast_to(jnp.sum(mine * mine, axis=1, keepdims=True), squares_ref.shape)


def finish(gram, left, w, nx):
    rank = gram.shape[0]
    nz, slab, _ = w.shape
    ranks = rank // nz
    rows = left.shape[0] // nx
    part = (slab - ranks // 2) // ranks * LANES
    vmem = pl.BlockSpec(memory_space=pltpu.VMEM)
    return pl.pallas_call(
        functools.partial(finish_kernel, nx),
        out_shape=(
            jax.ShapeDtypeStruct((nx, rows + ranks // nx, part), jnp.float32),
            jax.ShapeDtypeStruct((rows, rank), jnp.float32),
            jax.ShapeDtypeStruct((ranks, LANES), jnp.float32),
        ),
        in_specs=[vmem] * 3,
        out_specs=(vmem, vmem, vmem),
        scratch_shapes=[
            pltpu.VMEM((rank, rank), jnp.float32),
            pltpu.VMEM(left.shape, jnp.float32),
            pltpu.VMEM((rank, part), jnp.float32),
        ],
        compiler_params=pltpu.CompilerParams(vmem_limit_bytes=32 << 20),
        cost_estimate=pl.CostEstimate(
            flops=12 * rank**3 + 6 * left.shape[0] * rank * part, bytes_accessed=8 * left.shape[0] * part, transcendentals=256
        ),
    )(gram, left, w)


def on_device(momentum, gradient, basis):
    rows, columns = momentum.shape
    ranks = basis.shape[1]
    rank = 256
    nx, ny, nzh, nzl = lax.axis_size("x"), lax.axis_size("y"), lax.axis_size("zh"), lax.axis_size("zl")
    part = columns // nx
    own_ranks = nx * ranks
    peers = lax.axis_size(GROUP)

    v = lax.all_to_all(basis.T.reshape(ranks, nx, part).transpose(1, 0, 2), "x", 0, 0, tiled=True)
    buffer = split(momentum, gradient, nx)
    tall = lax.all_to_all(buffer, "x", 0, 0, tiled=True).reshape(nx * rows, part)
    v = lax.all_gather(v.reshape(own_ranks, part), Z, axis=0, tiled=True)

    partial = dot(tall, v, (1, 1))
    piece = partial.shape[0] // peers
    parts = lax.all_to_all(partial.reshape(peers, piece, rank), GROUP, 0, 0, tiled=True)
    own = jnp.sum(parts, axis=0)
    left = lax.all_to_all(jnp.broadcast_to(own[None], (peers, piece, rank)), GROUP, 0, 0, tiled=True)
    left = left.reshape(nx * rows, rank)

    both = sums(left, tall, nzh, nzl)
    slab = both.shape[1]
    both = lax.all_to_all(both, "zl", 0, 0, tiled=True)
    both = jnp.sum(both.reshape(nzl, nzh, slab, LANES), axis=0)
    both = jnp.sum(lax.all_to_all(both, "zh", 0, 0, tiled=True), axis=0)
    both = lax.all_gather(both, Z, axis=0)
    half = own_ranks // 2
    gram = both[:, slab - half :]
    gram = lax.all_to_all(jnp.broadcast_to(gram[None], (ny, *gram.shape)), "y", 0, 0, tiled=True)
    gram = gram.reshape(2, 2, nzh * nzl, half, LANES).transpose(2, 0, 3, 1, 4).reshape(rank, rank)

    back, orthonormal, squares = finish(gram, left, both, nx)
    squares = lax.psum(lax.psum(lax.psum(squares[:, 0], "core"), "y"), "x")
    squares = lax.dynamic_slice_in_dim(squares, lax.axis_index("x") * ranks, ranks, 0)
    back = lax.all_to_all(back, "x", 0, 0, tiled=True)
    new_momentum, new_basis = join(buffer, back, squares[:, None])
    new_basis = new_basis.T
    return (new_momentum, orthonormal, new_basis)


def solution(mesh):
    fine = Mesh(mesh.devices.reshape(4, 4, 4, 4, 2), ("zh", "zl", "x", "y", "core"))
    fsdp, tensor = ("zh", "zl", "x"), ("y", "core")
    return jax.shard_map(
        on_device,
        mesh=fine,
        in_specs=(P(fsdp, tensor), P(fsdp, tensor), P(tensor, fsdp)),
        out_specs=(P(fsdp, tensor), P(fsdp, None), P(tensor, fsdp)),
        check_vma=False,
    )
```

```python
import functools

import jax
import jax.numpy as jnp
from jax import lax
from jax.experimental import pallas as pl
from jax.experimental.pallas import tpu as pltpu
from jax.sharding import Mesh
from jax.sharding import PartitionSpec as P

momentum_keep = 0.95
column_eps = 1e-08
high = lax.Precision.HIGHEST

Z = ("zh", "zl")
GROUP = ("x", "y", "core")
HALF = 128
LANES = 128
SHIFT = 2
STEP = 8


def dot(a, b, contract, precision=high):
    return lax.dot_general(
        a, b, ((contract[:1], contract[1:]), ((), ())), precision=precision, preferred_element_type=jnp.float32
    )


def inverse_factor_block(block):
    n = block.shape[0]
    groups = [block[8 * g : 8 * g + 8, :] for g in range(n // 8)]
    lane = lax.broadcasted_iota(jnp.int32, (1, n), 1)
    row_in_group = lax.broadcasted_iota(jnp.int32, (8, n), 0)
    for k in range(0, n, STEP):
        first, at = k // 8, k % 8
        inside = (lane >= k) & (lane < k + STEP)
        cols = {
            g: [jnp.broadcast_to(groups[g][:, k + j : k + j + 1], (8, n)) for j in range(STEP)]
            for g in range(first, n // 8)
        }
        low = [[None] * STEP for _ in range(STEP)]
        inv = [[None] * STEP for _ in range(STEP)]
        a = [[cols[first][j][at + i : at + i + 1, :] for j in range(i + 1)] for i in range(STEP)]
        for j in range(STEP):
            inv[j][j] = lax.rsqrt(a[j][j])
            for i in range(j + 1, STEP):
                low[i][j] = a[i][j] * inv[j][j]
            for i in range(j + 1, STEP):
                for m in range(j + 1, i + 1):
                    a[i][m] = a[i][m] - low[i][j] * low[m][j]
        for j in range(STEP):
            for i in range(j + 1, STEP):
                value = low[i][j] * inv[j][j]
                for m in range(j + 1, i):
                    value = value + low[i][m] * inv[m][j]
                inv[i][j] = -(value * inv[i][i])
        rows = []
        for i in range(STEP):
            unit = jnp.where(lane == k + i, 1.0, 0.0)
            rows.append(jnp.where(inside, unit, groups[first][at + i : at + i + 1, :]))
        new = []
        for j in range(STEP):
            value = inv[j][0] * rows[0]
            for i in range(1, j + 1):
                value = value + inv[j][i] * rows[i]
            new.append(value)
        for g in range(first, n // 8):
            if g == first and at + STEP == 8:
                updated = groups[g]
            else:
                updated = jnp.where(inside, 0.0, groups[g])
                for j in range(STEP):
                    factor = inv[j][0] * cols[g][0]
                    for i in range(1, j + 1):
                        factor = factor + inv[j][i] * cols[g][i]
                    updated = updated - factor * new[j]
            if g == first:
                for j in range(STEP):
                    updated = jnp.where(row_in_group == at + j, new[j], updated)
            groups[g] = updated
    whole = jnp.concatenate(groups, axis=0)
    rows_at = lax.broadcasted_iota(jnp.int32, (n, n), 0)
    cols_at = lax.broadcasted_iota(jnp.int32, (n, n), 1)
    return jnp.where(rows_at >= cols_at, whole, 0.0)


def inverse_factor(gram):
    x11 = inverse_factor_block(gram[:HALF, :HALF])
    u = dot(x11, gram[:HALF, HALF:], (1, 0))
    rest = gram[HALF:, HALF:] - dot(u, u, (0, 0))
    t = dot(u, x11, (0, 0))
    x22 = inverse_factor_block(rest)
    return x11, -dot(x22, t, (1, 0)), x22


def split_kernel(momentum_ref, gradient_ref, out_ref):
    out_ref[0] = momentum_ref[...] + gradient_ref[...].astype(jnp.float32)


def split(momentum, gradient, parts):
    rows, columns = momentum.shape
    part = columns // parts
    block = pl.BlockSpec((rows, part), lambda i: (0, i))
    return pl.pallas_call(
        split_kernel,
        grid=(parts,),
        out_shape=jax.ShapeDtypeStruct((parts, rows, part), jnp.float32),
        in_specs=[block, block],
        out_specs=pl.BlockSpec((1, rows, part), lambda i: (i, 0, 0)),
        compiler_params=pltpu.CompilerParams(vmem_limit_bytes=16 << 20),
        cost_estimate=pl.CostEstimate(flops=momentum.size, bytes_accessed=10 * momentum.size, transcendentals=0),
    )(momentum, gradient)


def join_kernel(buffer_ref, back_ref, squares_ref, momentum_ref, basis_ref):
    parts, rows, part = buffer_ref.shape
    scale = 1.0 / (jnp.sqrt(squares_ref[...]) + column_eps)
    for i in range(parts):
        at = slice(i * part, (i + 1) * part)
        momentum_ref[:, at] = buffer_ref[i] - (1.0 - momentum_keep) * back_ref[i, :rows, :]
        basis_ref[:, at] = back_ref[i, rows:, :] * scale


def join(buffer, back, squares):
    parts, rows, part = buffer.shape
    ranks = back.shape[1] - rows
    vmem = pl.BlockSpec(memory_space=pltpu.VMEM)
    return pl.pallas_call(
        join_kernel,
        out_shape=(
            jax.ShapeDtypeStruct((rows, parts * part), jnp.float32),
            jax.ShapeDtypeStruct((ranks, parts * part), jnp.float32),
        ),
        in_specs=[vmem] * 3,
        out_specs=(vmem, vmem),
        compiler_params=pltpu.CompilerParams(vmem_limit_bytes=16 << 20),
        cost_estimate=pl.CostEstimate(flops=2 * buffer.size, bytes_accessed=12 * buffer.size, transcendentals=0),
    )(buffer, back, squares)


def sums_kernel(nzh, nzl, left_ref, tall_ref, out_ref, gram_ref):
    y_at, shift = lax.axis_index("y"), lax.axis_index("core") * SHIFT
    ranks = left_ref.shape[1] // (nzh * nzl)
    tiles = tall_ref.shape[1] // LANES
    left = left_ref[...]
    gram_ref[...] = dot(left, left, (0, 0))
    w = dot(left, tall_ref[...], (0, 0))
    half = ranks // 2
    lanes = pl.ds(pl.multiple_of((y_at % 2) * LANES, LANES), LANES)
    for z in range(nzh * nzl):
        line = (z + nzh * nzl - shift) % (nzh * nzl)
        at = (line % nzl) * nzh + line // nzl
        first = z * ranks
        for t in range(tiles):
            tile = w[first : first + ranks, t * LANES : (t + 1) * LANES]
            out_ref[pl.ds(at, 1), t * ranks : (t + 1) * ranks, :] = tile[None]
        piece = pl.ds(pl.multiple_of(first + (y_at // 2) * half, half), half)
        out_ref[pl.ds(at, 1), tiles * ranks :, :] = gram_ref[piece, lanes][None]


def sums(left, tall, nzh, nzl):
    rank, part = left.shape[1], tall.shape[1]
    ranks = rank // (nzh * nzl)
    rows = part // LANES * ranks + ranks // 2
    vmem = pl.BlockSpec(memory_space=pltpu.VMEM)
    return pl.pallas_call(
        functools.partial(sums_kernel, nzh, nzl),
        out_shape=jax.ShapeDtypeStruct((nzl * nzh, rows, LANES), jnp.float32),
        in_specs=[vmem, vmem],
        out_specs=vmem,
        scratch_shapes=[pltpu.VMEM((rank, rank), jnp.float32)],
        compiler_params=pltpu.CompilerParams(vmem_limit_bytes=24 << 20),
        cost_estimate=pl.CostEstimate(
            flops=12 * left.shape[0] * rank * (part + rank), bytes_accessed=4 * left.size + 8 * tall.size, transcendentals=0
        ),
    )(left, tall)


def finish_kernel(nx, gram_ref, left_ref, w_ref, back_ref, ortho_ref, squares_ref, inverse_ref, all_ref, right_ref):
    x_at, z_at = lax.axis_index("x"), lax.axis_index(Z)
    nz, slab, _ = w_ref.shape
    rank = inverse_ref.shape[0]
    ranks = rank // nz
    rows = left_ref.shape[0] // nx
    half = ranks // 2
    x11, x21, x22 = inverse_factor(gram_ref[...])
    inverse_ref[:HALF, :HALF] = x11
    inverse_ref[:HALF, HALF:] = jnp.zeros((HALF, HALF), jnp.float32)
    inverse_ref[HALF:, :HALF] = x21
    inverse_ref[HALF:, HALF:] = x22
    inverse = inverse_ref[...]
    tiles = (slab - half) // ranks
    for t in range(tiles):
        w = jnp.concatenate([w_ref[z, t * ranks : (t + 1) * ranks, :] for z in range(nz)], axis=0)
        right_ref[:, t * LANES : (t + 1) * LANES] = dot(inverse, w, (1, 0))
    all_ref[...] = dot(left_ref[...], inverse, (1, 1))
    ortho_ref[...] = all_ref[pl.ds(pl.multiple_of(x_at * rows, rows), rows), :]

    right = right_ref[...]
    right_high = right.astype(jnp.bfloat16)
    right_low = (right - right_high.astype(jnp.float32)).astype(jnp.bfloat16)
    for x in range(nx):
        q = all_ref[x * rows : (x + 1) * rows, :]
        q_high = q.astype(jnp.bfloat16)
        q_low = (q - q_high.astype(jnp.float32)).astype(jnp.bfloat16)
        plain = lax.Precision.DEFAULT
        small = dot(q_low, right_high, (1, 0), plain) + dot(q_high, right_low, (1, 0), plain)
        back_ref[x, :rows, :] = small + dot(q_high, right_high, (1, 0), plain)
    mine = right_ref[pl.ds(pl.multiple_of(z_at * ranks, ranks), ranks), :]
    each = ranks // nx
    for x in range(nx):
        back_ref[x, rows : rows + each, :] = mine[x * each : (x + 1) * each, :]
    squares_ref[...] = jnp.broadcast_to(jnp.sum(mine * mine, axis=1, keepdims=True), squares_ref.shape)


def finish(gram, left, w, nx):
    rank = gram.shape[0]
    nz, slab, _ = w.shape
    ranks = rank // nz
    rows = left.shape[0] // nx
    part = (slab - ranks // 2) // ranks * LANES
    vmem = pl.BlockSpec(memory_space=pltpu.VMEM)
    return pl.pallas_call(
        functools.partial(finish_kernel, nx),
        out_shape=(
            jax.ShapeDtypeStruct((nx, rows + ranks // nx, part), jnp.float32),
            jax.ShapeDtypeStruct((rows, rank), jnp.float32),
            jax.ShapeDtypeStruct((ranks, LANES), jnp.float32),
        ),
        in_specs=[vmem] * 3,
        out_specs=(vmem, vmem, vmem),
        scratch_shapes=[
            pltpu.VMEM((rank, rank), jnp.float32),
            pltpu.VMEM(left.shape, jnp.float32),
            pltpu.VMEM((rank, part), jnp.float32),
        ],
        compiler_params=pltpu.CompilerParams(vmem_limit_bytes=32 << 20),
        cost_estimate=pl.CostEstimate(
            flops=12 * rank**3 + 6 * left.shape[0] * rank * part, bytes_accessed=8 * left.shape[0] * part, transcendentals=256
        ),
    )(gram, left, w)


def z_groups(nzh, nzl, cores):
    nz = nzh * nzl
    near, far = [], []
    for core in range(cores):
        at = [[((zh * nzl + zl + SHIFT * core) % nz) * cores + core for zl in range(nzl)] for zh in range(nzh)]
        near += at
        far += [list(group) for group in zip(*at)]
    return near, far


def on_device(momentum, gradient, basis):
    rows, columns = momentum.shape
    ranks = basis.shape[1]
    rank = 256
    nx, ny, nzh, nzl = lax.axis_size("x"), lax.axis_size("y"), lax.axis_size("zh"), lax.axis_size("zl")
    part = columns // nx
    own_ranks = nx * ranks
    peers = lax.axis_size(GROUP)

    v = lax.all_to_all(basis.T.reshape(ranks, nx, part).transpose(1, 0, 2), "x", 0, 0, tiled=True)
    buffer = split(momentum, gradient, nx)
    tall = lax.all_to_all(buffer, "x", 0, 0, tiled=True).reshape(nx * rows, part)
    v = lax.all_gather(v.reshape(own_ranks, part), Z, axis=0, tiled=True)

    partial = dot(tall, v, (1, 1))
    piece = partial.shape[0] // peers
    parts = lax.all_to_all(partial.reshape(peers, piece, rank), GROUP, 0, 0, tiled=True)
    own = jnp.sum(parts, axis=0)
    left = lax.all_to_all(jnp.broadcast_to(own[None], (peers, piece, rank)), GROUP, 0, 0, tiled=True)
    left = left.reshape(nx * rows, rank)

    both = sums(left, tall, nzh, nzl)
    slab = both.shape[1]
    lines = (*Z, "core")
    near, far = z_groups(nzh, nzl, lax.axis_size("core"))
    both = lax.all_to_all(both, lines, 0, 0, tiled=True, axis_index_groups=near)
    both = jnp.sum(both.reshape(nzl, nzh, slab, LANES), axis=0)
    both = jnp.sum(lax.all_to_all(both, lines, 0, 0, tiled=True, axis_index_groups=far), axis=0)
    both = lax.all_gather(both, Z, axis=0)
    half = own_ranks // 2
    gram = both[:, slab - half :]
    gram = lax.all_to_all(jnp.broadcast_to(gram[None], (ny, *gram.shape)), "y", 0, 0, tiled=True)
    gram = gram.reshape(2, 2, nzh * nzl, half, LANES).transpose(2, 0, 3, 1, 4).reshape(rank, rank)

    back, orthonormal, squares = finish(gram, left, both, nx)
    squares = lax.psum(lax.psum(lax.psum(squares[:, 0], "core"), "y"), "x")
    squares = lax.dynamic_slice_in_dim(squares, lax.axis_index("x") * ranks, ranks, 0)
    back = lax.all_to_all(back, "x", 0, 0, tiled=True)
    new_momentum, new_basis = join(buffer, back, squares[:, None])
    new_basis = new_basis.T
    return (new_momentum, orthonormal, new_basis)


def solution(mesh):
    fine = Mesh(mesh.devices.reshape(4, 4, 4, 4, 2), ("zh", "zl", "x", "y", "core"))
    fsdp, tensor = ("zh", "zl", "x"), ("y", "core")
    return jax.shard_map(
        on_device,
        mesh=fine,
        in_specs=(P(fsdp, tensor), P(fsdp, tensor), P(tensor, fsdp)),
        out_specs=(P(fsdp, tensor), P(fsdp, None), P(tensor, fsdp)),
        check_vma=False,
    )
```

```python
import functools

import jax
import jax.numpy as jnp
from jax import lax
from jax.experimental import pallas as pl
from jax.experimental.pallas import tpu as pltpu
from jax.sharding import Mesh
from jax.sharding import PartitionSpec as P

momentum_keep = 0.95
column_eps = 1e-08
high = lax.Precision.HIGHEST

Z = ("zh", "zl")
GROUP = ("x", "y", "core")
HALF = 128
QUARTER = 64
REST = 7 * QUARTER // 4
LANES = 128
SHIFT = 2
STEP = 8


def dot(a, b, contract, precision=high):
    return lax.dot_general(
        a, b, ((contract[:1], contract[1:]), ((), ())), precision=precision, preferred_element_type=jnp.float32
    )


def inverse_factor_block(block):
    n = block.shape[0]
    groups = [block[8 * g : 8 * g + 8, :] for g in range(n // 8)]
    lane = lax.broadcasted_iota(jnp.int32, (1, n), 1)
    row_in_group = lax.broadcasted_iota(jnp.int32, (8, n), 0)
    for k in range(0, n, STEP):
        first, at = k // 8, k % 8
        inside = (lane >= k) & (lane < k + STEP)
        cols = {
            g: [jnp.broadcast_to(groups[g][:, k + j : k + j + 1], (8, n)) for j in range(STEP)]
            for g in range(first, n // 8)
        }
        low = [[None] * STEP for _ in range(STEP)]
        inv = [[None] * STEP for _ in range(STEP)]
        a = [[cols[first][j][at + i : at + i + 1, :] for j in range(i + 1)] for i in range(STEP)]
        for j in range(STEP):
            inv[j][j] = lax.rsqrt(a[j][j])
            for i in range(j + 1, STEP):
                low[i][j] = a[i][j] * inv[j][j]
            for i in range(j + 1, STEP):
                for m in range(j + 1, i + 1):
                    a[i][m] = a[i][m] - low[i][j] * low[m][j]
        for j in range(STEP):
            for i in range(j + 1, STEP):
                value = low[i][j] * inv[j][j]
                for m in range(j + 1, i):
                    value = value + low[i][m] * inv[m][j]
                inv[i][j] = -(value * inv[i][i])
        rows = []
        for i in range(STEP):
            unit = jnp.where(lane == k + i, 1.0, 0.0)
            rows.append(jnp.where(inside, unit, groups[first][at + i : at + i + 1, :]))
        new = []
        for j in range(STEP):
            value = inv[j][0] * rows[0]
            for i in range(1, j + 1):
                value = value + inv[j][i] * rows[i]
            new.append(value)
        for g in range(first, n // 8):
            if g == first and at + STEP == 8:
                updated = groups[g]
            else:
                updated = jnp.where(inside, 0.0, groups[g])
                for j in range(STEP):
                    factor = inv[j][0] * cols[g][0]
                    for i in range(1, j + 1):
                        factor = factor + inv[j][i] * cols[g][i]
                    updated = updated - factor * new[j]
            if g == first:
                for j in range(STEP):
                    updated = jnp.where(row_in_group == at + j, new[j], updated)
            groups[g] = updated
    whole = jnp.concatenate(groups, axis=0)
    rows_at = lax.broadcasted_iota(jnp.int32, (n, n), 0)
    cols_at = lax.broadcasted_iota(jnp.int32, (n, n), 1)
    return jnp.where(rows_at >= cols_at, whole, 0.0)


def split_kernel(momentum_ref, gradient_ref, out_ref):
    out_ref[0] = momentum_ref[...] + gradient_ref[...].astype(jnp.float32)


def split(momentum, gradient, parts):
    rows, columns = momentum.shape
    part = columns // parts
    block = pl.BlockSpec((rows, part), lambda i: (0, i))
    return pl.pallas_call(
        split_kernel,
        grid=(parts,),
        out_shape=jax.ShapeDtypeStruct((parts, rows, part), jnp.float32),
        in_specs=[block, block],
        out_specs=pl.BlockSpec((1, rows, part), lambda i: (i, 0, 0)),
        compiler_params=pltpu.CompilerParams(vmem_limit_bytes=16 << 20),
        cost_estimate=pl.CostEstimate(flops=momentum.size, bytes_accessed=10 * momentum.size, transcendentals=0),
    )(momentum, gradient)


def join_kernel(buffer_ref, back_ref, squares_ref, momentum_ref, basis_ref):
    parts, rows, part = buffer_ref.shape
    scale = 1.0 / (jnp.sqrt(squares_ref[...]) + column_eps)
    for i in range(parts):
        at = slice(i * part, (i + 1) * part)
        momentum_ref[:, at] = buffer_ref[i] - (1.0 - momentum_keep) * back_ref[i, :rows, :]
        basis_ref[:, at] = back_ref[i, rows:, :] * scale


def join(buffer, back, squares):
    parts, rows, part = buffer.shape
    ranks = back.shape[1] - rows
    vmem = pl.BlockSpec(memory_space=pltpu.VMEM)
    return pl.pallas_call(
        join_kernel,
        out_shape=(
            jax.ShapeDtypeStruct((rows, parts * part), jnp.float32),
            jax.ShapeDtypeStruct((ranks, parts * part), jnp.float32),
        ),
        in_specs=[vmem] * 3,
        out_specs=(vmem, vmem),
        compiler_params=pltpu.CompilerParams(vmem_limit_bytes=16 << 20),
        cost_estimate=pl.CostEstimate(flops=2 * buffer.size, bytes_accessed=12 * buffer.size, transcendentals=0),
    )(buffer, back, squares)


def sums_kernel(nzh, nzl, left_ref, tall_ref, out_ref, gram_ref, rest_ref):
    core_at = lax.axis_index("core")
    shift = core_at * SHIFT
    ranks = left_ref.shape[1] // (nzh * nzl)
    tiles = tall_ref.shape[1] // LANES
    left = left_ref[...]
    gram_ref[...] = dot(left, left, (0, 0))
    w = dot(left, tall_ref[...], (0, 0))
    first_rows, rest_rows = HALF // (nzh * nzl), REST // (nzh * nzl)
    rest_ref[:HALF, :] = gram_ref[:HALF, HALF:]
    rest_ref[HALF : HALF + QUARTER, :] = gram_ref[HALF + QUARTER :, HALF:]
    corner = gram_ref[HALF : HALF + QUARTER, HALF : HALF + QUARTER]
    rest_ref[HALF + QUARTER :, :] = jnp.concatenate([corner[: QUARTER // 2], corner[QUARTER // 2 :]], axis=1)
    rest = rest_ref[pl.ds(pl.multiple_of(core_at * REST, 8), REST), :]
    for z in range(nzh * nzl):
        line = (z + nzh * nzl - shift) % (nzh * nzl)
        at = (line % nzl) * nzh + line // nzl
        first = z * ranks
        for t in range(tiles):
            tile = w[first : first + ranks, t * LANES : (t + 1) * LANES]
            out_ref[pl.ds(at, 1), t * ranks : (t + 1) * ranks, :] = tile[None]
        end = tiles * ranks + first_rows
        out_ref[pl.ds(at, 1), tiles * ranks : end, :] = gram_ref[z * first_rows : (z + 1) * first_rows, :HALF][None]
        out_ref[pl.ds(at, 1), end:, :] = rest[z * rest_rows : (z + 1) * rest_rows][None]


def sums(left, tall, nzh, nzl):
    rank, part = left.shape[1], tall.shape[1]
    ranks = rank // (nzh * nzl)
    rows = part // LANES * ranks + (HALF + REST) // (nzh * nzl)
    vmem = pl.BlockSpec(memory_space=pltpu.VMEM)
    return pl.pallas_call(
        functools.partial(sums_kernel, nzh, nzl),
        out_shape=jax.ShapeDtypeStruct((nzl * nzh, rows, LANES), jnp.float32),
        in_specs=[vmem, vmem],
        out_specs=vmem,
        scratch_shapes=[pltpu.VMEM((rank, rank), jnp.float32), pltpu.VMEM((2 * REST, LANES), jnp.float32)],
        compiler_params=pltpu.CompilerParams(vmem_limit_bytes=24 << 20),
        cost_estimate=pl.CostEstimate(
            flops=12 * left.shape[0] * rank * (part + rank), bytes_accessed=4 * left.size + 8 * tall.size, transcendentals=0
        ),
    )(left, tall)


def product_in_parts(a, b):
    a_high, b_high = a.astype(jnp.bfloat16), b.astype(jnp.bfloat16)
    a_low = (a - a_high.astype(jnp.float32)).astype(jnp.bfloat16)
    b_low = (b - b_high.astype(jnp.float32)).astype(jnp.bfloat16)
    plain = lax.Precision.DEFAULT
    small = dot(a_low, b_high, (1, 0), plain) + dot(a_high, b_low, (1, 0), plain)
    return small + dot(a_high, b_high, (1, 0), plain)


def w_rows(w_ref, first, tiles, ranks):
    slabs = range(first // ranks, (first + HALF) // ranks)
    parts = [jnp.concatenate([w_ref[z, t * ranks : (t + 1) * ranks, :] for z in slabs], axis=0) for t in range(tiles)]
    return jnp.concatenate(parts, axis=1)


def first_kernel(tiles, ranks, w_ref, left_ref, x11_ref, right_ref, ortho_ref):
    rows = HALF // w_ref.shape[0]
    block = jnp.concatenate(
        [w_ref[z, tiles * ranks : tiles * ranks + rows, :] for z in range(w_ref.shape[0])], axis=0
    )
    x11 = inverse_factor_block(block)
    x11_ref[...] = x11
    right_ref[...] = dot(x11, w_rows(w_ref, 0, tiles, ranks), (1, 0))
    ortho_ref[...] = dot(left_ref[:, :HALF], x11, (1, 1))


def finish_kernel(
    nx, tiles, ranks, mine_ref, other_ref, w_ref, left_ref, x11_ref, right_one_ref, ortho_one_ref, back_ref, ortho_ref, squares_ref, all_ref, right_ref
):
    x_at, z_at = lax.axis_index("x"), lax.axis_index(Z)
    rows = left_ref.shape[0] // nx
    x11 = x11_ref[...]
    is_first = lax.axis_index("core") == 0
    mine = jnp.concatenate([mine_ref[z] for z in range(mine_ref.shape[0])], axis=0)
    other = jnp.concatenate([other_ref[z] for z in range(other_ref.shape[0])], axis=0)
    rest = jnp.concatenate([jnp.where(is_first, mine, other), jnp.where(is_first, other, mine)], axis=0)
    folded = rest[HALF + QUARTER :]
    corner = jnp.concatenate([folded[:, :QUARTER], folded[:, QUARTER:]], axis=0)
    upper = jnp.concatenate([corner, jnp.zeros((QUARTER, QUARTER), jnp.float32)], axis=1)
    lower = jnp.concatenate([upper, rest[HALF : HALF + QUARTER]], axis=0)
    right_upper = (lax.broadcasted_iota(jnp.int32, (HALF, HALF), 1) >= QUARTER) & (
        lax.broadcasted_iota(jnp.int32, (HALF, HALF), 0) < QUARTER
    )
    u = dot(x11, rest[:HALF], (1, 0))
    x22 = inverse_factor_block(jnp.where(right_upper, lower.T, lower) - dot(u, u, (0, 0)))
    x21 = -dot(x22, dot(u, x11, (0, 0)), (1, 0))
    right_ref[:HALF, :] = right_one_ref[...]
    all_ref[:, :HALF] = ortho_one_ref[...]
    right_ref[HALF:, :] = dot(x21, w_rows(w_ref, 0, tiles, ranks), (1, 0)) + dot(
        x22, w_rows(w_ref, HALF, tiles, ranks), (1, 0)
    )
    all_ref[:, HALF:] = dot(left_ref[:, :HALF], x21, (1, 1)) + dot(left_ref[:, HALF:], x22, (1, 1))
    for x in range(nx):
        back_ref[x, :rows, :] = product_in_parts(all_ref[x * rows : (x + 1) * rows, :], right_ref[...])
    ortho_ref[...] = all_ref[pl.ds(pl.multiple_of(x_at * rows, rows), rows), :]
    mine = right_ref[pl.ds(pl.multiple_of(z_at * ranks, ranks), ranks), :]
    each = ranks // nx
    for x in range(nx):
        back_ref[x, rows : rows + each, :] = mine[x * each : (x + 1) * each, :]
    squares_ref[...] = jnp.broadcast_to(jnp.sum(mine * mine, axis=1, keepdims=True), squares_ref.shape)


def first(w, left, tiles, ranks):
    vmem = pl.BlockSpec(memory_space=pltpu.VMEM)
    part = tiles * LANES
    return pl.pallas_call(
        functools.partial(first_kernel, tiles, ranks),
        out_shape=(
            jax.ShapeDtypeStruct((HALF, HALF), jnp.float32),
            jax.ShapeDtypeStruct((HALF, part), jnp.float32),
            jax.ShapeDtypeStruct((left.shape[0], HALF), jnp.float32),
        ),
        in_specs=[vmem] * 2,
        out_specs=(vmem,) * 3,
        compiler_params=pltpu.CompilerParams(vmem_limit_bytes=16 << 20),
        cost_estimate=pl.CostEstimate(flops=12 * HALF**2 * (part + left.shape[0]), bytes_accessed=8 * w.size, transcendentals=HALF),
    )(w, left)


def finish(mine, other, w, left, one, nx, tiles, ranks):
    rank = left.shape[1]
    rows, part = left.shape[0] // nx, tiles * LANES
    vmem = pl.BlockSpec(memory_space=pltpu.VMEM)
    return pl.pallas_call(
        functools.partial(finish_kernel, nx, tiles, ranks),
        out_shape=(
            jax.ShapeDtypeStruct((nx, rows + ranks // nx, part), jnp.float32),
            jax.ShapeDtypeStruct((rows, rank), jnp.float32),
            jax.ShapeDtypeStruct((ranks, LANES), jnp.float32),
        ),
        in_specs=[vmem] * 7,
        out_specs=(vmem,) * 3,
        scratch_shapes=[pltpu.VMEM(left.shape, jnp.float32), pltpu.VMEM((rank, part), jnp.float32)],
        compiler_params=pltpu.CompilerParams(vmem_limit_bytes=32 << 20),
        cost_estimate=pl.CostEstimate(
            flops=12 * rank**3 + 6 * left.shape[0] * rank * part, bytes_accessed=8 * left.shape[0] * part, transcendentals=HALF
        ),
    )(mine, other, w, left, *one)


def z_groups(nzh, nzl, cores):
    nz = nzh * nzl
    near, far = [], []
    for core in range(cores):
        at = [[((zh * nzl + zl + SHIFT * core) % nz) * cores + core for zl in range(nzl)] for zh in range(nzh)]
        near += at
        far += [list(group) for group in zip(*at)]
    return near, far


def on_device(momentum, gradient, basis):
    rows, columns = momentum.shape
    ranks = basis.shape[1]
    rank = 256
    nx, nzh, nzl = lax.axis_size("x"), lax.axis_size("zh"), lax.axis_size("zl")
    part = columns // nx
    own_ranks = nx * ranks
    peers = lax.axis_size(GROUP)

    v = lax.all_to_all(basis.T.reshape(ranks, nx, part).transpose(1, 0, 2), "x", 0, 0, tiled=True)
    buffer = split(momentum, gradient, nx)
    tall = lax.all_to_all(buffer, "x", 0, 0, tiled=True).reshape(nx * rows, part)
    v = lax.all_gather(v.reshape(own_ranks, part), Z, axis=0, tiled=True)

    partial = dot(tall, v, (1, 1))
    piece = partial.shape[0] // peers
    parts = lax.all_to_all(partial.reshape(peers, piece, rank), GROUP, 0, 0, tiled=True)
    own = jnp.sum(parts, axis=0)
    left = lax.all_to_all(jnp.broadcast_to(own[None], (peers, piece, rank)), GROUP, 0, 0, tiled=True)
    left = left.reshape(nx * rows, rank)

    both = sums(left, tall, nzh, nzl)
    slab = both.shape[1]
    lines = (*Z, "core")
    near, far = z_groups(nzh, nzl, lax.axis_size("core"))
    both = lax.all_to_all(both, lines, 0, 0, tiled=True, axis_index_groups=near)
    both = jnp.sum(both.reshape(nzl, nzh, slab, LANES), axis=0)
    both = jnp.sum(lax.all_to_all(both, lines, 0, 0, tiled=True, axis_index_groups=far), axis=0)
    both = lax.all_gather(both, Z, axis=0)
    tiles = part // LANES
    rest = both[:, slab - REST // (nzh * nzl) :]
    other = lax.ppermute(rest, "core", [(0, 1), (1, 0)])
    one = first(both, left, tiles, own_ranks)

    back, orthonormal, squares = finish(rest, other, both, left, one, nx, tiles, own_ranks)
    squares = lax.psum(lax.psum(lax.psum(squares[:, 0], "core"), "y"), "x")
    squares = lax.dynamic_slice_in_dim(squares, lax.axis_index("x") * ranks, ranks, 0)
    back = lax.all_to_all(back, "x", 0, 0, tiled=True)
    new_momentum, new_basis = join(buffer, back, squares[:, None])
    new_basis = new_basis.T
    return (new_momentum, orthonormal, new_basis)


def solution(mesh):
    fine = Mesh(mesh.devices.reshape(4, 4, 4, 4, 2), ("zh", "zl", "x", "y", "core"))
    fsdp, tensor = ("zh", "zl", "x"), ("y", "core")
    return jax.shard_map(
        on_device,
        mesh=fine,
        in_specs=(P(fsdp, tensor), P(fsdp, tensor), P(tensor, fsdp)),
        out_specs=(P(fsdp, tensor), P(fsdp, None), P(tensor, fsdp)),
        check_vma=False,
    )
```

```python
import functools

import jax
import jax.numpy as jnp
from jax import lax
from jax.experimental import pallas as pl
from jax.experimental.pallas import tpu as pltpu
from jax.sharding import Mesh
from jax.sharding import PartitionSpec as P

momentum_keep = 0.95
column_eps = 1e-08
high = lax.Precision.HIGHEST

Z = ("zh", "zl")
GROUP = ("x", "y", "core")
HALF = 128
LANES = 128
SHIFT = 2
STEP = 8


def dot(a, b, contract, precision=high):
    return lax.dot_general(
        a, b, ((contract[:1], contract[1:]), ((), ())), precision=precision, preferred_element_type=jnp.float32
    )


def inverse_factor_block(block):
    n = block.shape[0]
    groups = [block[8 * g : 8 * g + 8, :] for g in range(n // 8)]
    lane = lax.broadcasted_iota(jnp.int32, (1, n), 1)
    row_in_group = lax.broadcasted_iota(jnp.int32, (8, n), 0)
    for k in range(0, n, STEP):
        first, at = k // 8, k % 8
        inside = (lane >= k) & (lane < k + STEP)
        cols = {
            g: [jnp.broadcast_to(groups[g][:, k + j : k + j + 1], (8, n)) for j in range(STEP)]
            for g in range(first, n // 8)
        }
        low = [[None] * STEP for _ in range(STEP)]
        inv = [[None] * STEP for _ in range(STEP)]
        a = [[cols[first][j][at + i : at + i + 1, :] for j in range(i + 1)] for i in range(STEP)]
        for j in range(STEP):
            inv[j][j] = lax.rsqrt(a[j][j])
            for i in range(j + 1, STEP):
                low[i][j] = a[i][j] * inv[j][j]
            for i in range(j + 1, STEP):
                for m in range(j + 1, i + 1):
                    a[i][m] = a[i][m] - low[i][j] * low[m][j]
        for j in range(STEP):
            for i in range(j + 1, STEP):
                value = low[i][j] * inv[j][j]
                for m in range(j + 1, i):
                    value = value + low[i][m] * inv[m][j]
                inv[i][j] = -(value * inv[i][i])
        rows = []
        for i in range(STEP):
            unit = jnp.where(lane == k + i, 1.0, 0.0)
            rows.append(jnp.where(inside, unit, groups[first][at + i : at + i + 1, :]))
        new = []
        for j in range(STEP):
            value = inv[j][0] * rows[0]
            for i in range(1, j + 1):
                value = value + inv[j][i] * rows[i]
            new.append(value)
        for g in range(first, n // 8):
            if g == first and at + STEP == 8:
                updated = groups[g]
            else:
                updated = jnp.where(inside, 0.0, groups[g])
                for j in range(STEP):
                    factor = inv[j][0] * cols[g][0]
                    for i in range(1, j + 1):
                        factor = factor + inv[j][i] * cols[g][i]
                    updated = updated - factor * new[j]
            if g == first:
                for j in range(STEP):
                    updated = jnp.where(row_in_group == at + j, new[j], updated)
            groups[g] = updated
    whole = jnp.concatenate(groups, axis=0)
    rows_at = lax.broadcasted_iota(jnp.int32, (n, n), 0)
    cols_at = lax.broadcasted_iota(jnp.int32, (n, n), 1)
    return jnp.where(rows_at >= cols_at, whole, 0.0)


def inverse_factor(gram):
    x11 = inverse_factor_block(gram[:HALF, :HALF])
    u = dot(x11, gram[:HALF, HALF:], (1, 0))
    rest = gram[HALF:, HALF:] - dot(u, u, (0, 0))
    t = dot(u, x11, (0, 0))
    x22 = inverse_factor_block(rest)
    return x11, -dot(x22, t, (1, 0)), x22


def split_kernel(momentum_ref, gradient_ref, out_ref):
    out_ref[0] = momentum_ref[...] + gradient_ref[...].astype(jnp.float32)


def split(momentum, gradient, parts):
    rows, columns = momentum.shape
    part = columns // parts
    block = pl.BlockSpec((rows, part), lambda i: (0, i))
    return pl.pallas_call(
        split_kernel,
        grid=(parts,),
        out_shape=jax.ShapeDtypeStruct((parts, rows, part), jnp.float32),
        in_specs=[block, block],
        out_specs=pl.BlockSpec((1, rows, part), lambda i: (i, 0, 0)),
        compiler_params=pltpu.CompilerParams(vmem_limit_bytes=16 << 20),
        cost_estimate=pl.CostEstimate(flops=momentum.size, bytes_accessed=10 * momentum.size, transcendentals=0),
    )(momentum, gradient)


def join_kernel(buffer_ref, back_ref, momentum_ref, basis_ref):
    parts, rows, part = buffer_ref.shape
    for i in range(parts):
        at = slice(i * part, (i + 1) * part)
        momentum_ref[:, at] = buffer_ref[i] - (1.0 - momentum_keep) * back_ref[i, :rows, :]
        basis_ref[:, at] = back_ref[i, rows:, :]


def join(buffer, back):
    parts, rows, part = buffer.shape
    ranks = back.shape[1] - rows
    vmem = pl.BlockSpec(memory_space=pltpu.VMEM)
    return pl.pallas_call(
        join_kernel,
        out_shape=(
            jax.ShapeDtypeStruct((rows, parts * part), jnp.float32),
            jax.ShapeDtypeStruct((ranks, parts * part), jnp.float32),
        ),
        in_specs=[vmem] * 2,
        out_specs=(vmem, vmem),
        compiler_params=pltpu.CompilerParams(vmem_limit_bytes=16 << 20),
        cost_estimate=pl.CostEstimate(flops=2 * buffer.size, bytes_accessed=12 * buffer.size, transcendentals=0),
    )(buffer, back)


def sums_kernel(nzh, nzl, left_ref, tall_ref, out_ref, gram_ref):
    y_at, shift = lax.axis_index("y"), lax.axis_index("core") * SHIFT
    ranks = left_ref.shape[1] // (nzh * nzl)
    tiles = tall_ref.shape[1] // LANES
    left = left_ref[...]
    gram_ref[...] = dot(left, left, (0, 0))
    w = dot(left, tall_ref[...], (0, 0))
    half = ranks // 2
    lanes = pl.ds(pl.multiple_of((y_at % 2) * LANES, LANES), LANES)
    for z in range(nzh * nzl):
        line = (z + nzh * nzl - shift) % (nzh * nzl)
        at = (line % nzl) * nzh + line // nzl
        first = z * ranks
        for t in range(tiles):
            tile = w[first : first + ranks, t * LANES : (t + 1) * LANES]
            out_ref[pl.ds(at, 1), t * ranks : (t + 1) * ranks, :] = tile[None]
        piece = pl.ds(pl.multiple_of(first + (y_at // 2) * half, half), half)
        out_ref[pl.ds(at, 1), tiles * ranks :, :] = gram_ref[piece, lanes][None]


def sums(left, tall, nzh, nzl):
    rank, part = left.shape[1], tall.shape[1]
    ranks = rank // (nzh * nzl)
    rows = part // LANES * ranks + ranks // 2
    vmem = pl.BlockSpec(memory_space=pltpu.VMEM)
    return pl.pallas_call(
        functools.partial(sums_kernel, nzh, nzl),
        out_shape=jax.ShapeDtypeStruct((nzl * nzh, rows, LANES), jnp.float32),
        in_specs=[vmem, vmem],
        out_specs=vmem,
        scratch_shapes=[pltpu.VMEM((rank, rank), jnp.float32)],
        compiler_params=pltpu.CompilerParams(vmem_limit_bytes=24 << 20),
        cost_estimate=pl.CostEstimate(
            flops=12 * left.shape[0] * rank * (part + rank), bytes_accessed=4 * left.size + 8 * tall.size, transcendentals=0
        ),
    )(left, tall)


def finish_kernel(nx, gram_ref, left_ref, w_ref, back_ref, ortho_ref, squares_ref, inverse_ref, all_ref, right_ref):
    x_at, z_at = lax.axis_index("x"), lax.axis_index(Z)
    nz, slab, _ = w_ref.shape
    rank = inverse_ref.shape[0]
    ranks = rank // nz
    rows = left_ref.shape[0] // nx
    half = ranks // 2
    x11, x21, x22 = inverse_factor(gram_ref[...])
    inverse_ref[:HALF, :HALF] = x11
    inverse_ref[:HALF, HALF:] = jnp.zeros((HALF, HALF), jnp.float32)
    inverse_ref[HALF:, :HALF] = x21
    inverse_ref[HALF:, HALF:] = x22
    inverse = inverse_ref[...]
    tiles = (slab - half) // ranks
    for t in range(tiles):
        w = jnp.concatenate([w_ref[z, t * ranks : (t + 1) * ranks, :] for z in range(nz)], axis=0)
        right_ref[:, t * LANES : (t + 1) * LANES] = dot(inverse, w, (1, 0))
    all_ref[...] = dot(left_ref[...], inverse, (1, 1))
    ortho_ref[...] = all_ref[pl.ds(pl.multiple_of(x_at * rows, rows), rows), :]

    right = right_ref[...]
    right_high = right.astype(jnp.bfloat16)
    right_low = (right - right_high.astype(jnp.float32)).astype(jnp.bfloat16)
    for x in range(nx):
        q = all_ref[x * rows : (x + 1) * rows, :]
        q_high = q.astype(jnp.bfloat16)
        q_low = (q - q_high.astype(jnp.float32)).astype(jnp.bfloat16)
        plain = lax.Precision.DEFAULT
        small = dot(q_low, right_high, (1, 0), plain) + dot(q_high, right_low, (1, 0), plain)
        back_ref[x, :rows, :] = small + dot(q_high, right_high, (1, 0), plain)
    mine = right_ref[pl.ds(pl.multiple_of(z_at * ranks, ranks), ranks), :]
    each = ranks // nx
    for x in range(nx):
        back_ref[x, rows : rows + each, :] = mine[x * each : (x + 1) * each, :]
    squares_ref[...] = jnp.broadcast_to(jnp.sum(mine * mine, axis=1, keepdims=True), squares_ref.shape)


def finish(gram, left, w, nx):
    rank = gram.shape[0]
    nz, slab, _ = w.shape
    ranks = rank // nz
    rows = left.shape[0] // nx
    part = (slab - ranks // 2) // ranks * LANES
    vmem = pl.BlockSpec(memory_space=pltpu.VMEM)
    return pl.pallas_call(
        functools.partial(finish_kernel, nx),
        out_shape=(
            jax.ShapeDtypeStruct((nx, rows + ranks // nx, part), jnp.float32),
            jax.ShapeDtypeStruct((rows, rank), jnp.float32),
            jax.ShapeDtypeStruct((ranks, LANES), jnp.float32),
        ),
        in_specs=[vmem] * 3,
        out_specs=(vmem, vmem, vmem),
        scratch_shapes=[
            pltpu.VMEM((rank, rank), jnp.float32),
            pltpu.VMEM(left.shape, jnp.float32),
            pltpu.VMEM((rank, part), jnp.float32),
        ],
        compiler_params=pltpu.CompilerParams(vmem_limit_bytes=32 << 20),
        cost_estimate=pl.CostEstimate(
            flops=12 * rank**3 + 6 * left.shape[0] * rank * part, bytes_accessed=8 * left.shape[0] * part, transcendentals=256
        ),
    )(gram, left, w)


def z_groups(nzh, nzl, cores):
    nz = nzh * nzl
    near, far = [], []
    for core in range(cores):
        at = [[((zh * nzl + zl + SHIFT * core) % nz) * cores + core for zl in range(nzl)] for zh in range(nzh)]
        near += at
        far += [list(group) for group in zip(*at)]
    return near, far


def on_device(momentum, gradient, basis):
    rows, columns = momentum.shape
    ranks = basis.shape[1]
    rank = 256
    nx, ny, nzh, nzl = lax.axis_size("x"), lax.axis_size("y"), lax.axis_size("zh"), lax.axis_size("zl")
    part = columns // nx
    own_ranks = nx * ranks
    peers = lax.axis_size(GROUP)

    v = lax.all_to_all(basis.T.reshape(ranks, nx, part).transpose(1, 0, 2), "x", 0, 0, tiled=True)
    buffer = split(momentum, gradient, nx)
    tall = lax.all_to_all(buffer, "x", 0, 0, tiled=True).reshape(nx * rows, part)
    v = lax.all_gather(v.reshape(own_ranks, part), Z, axis=0, tiled=True)

    partial = dot(tall, v, (1, 1))
    piece = partial.shape[0] // peers
    parts = lax.all_to_all(partial.reshape(peers, piece, rank), GROUP, 0, 0, tiled=True)
    own = jnp.sum(parts, axis=0)
    left = lax.all_to_all(jnp.broadcast_to(own[None], (peers, piece, rank)), GROUP, 0, 0, tiled=True)
    left = left.reshape(nx * rows, rank)

    both = sums(left, tall, nzh, nzl)
    slab = both.shape[1]
    lines = (*Z, "core")
    near, far = z_groups(nzh, nzl, lax.axis_size("core"))
    both = lax.all_to_all(both, lines, 0, 0, tiled=True, axis_index_groups=near)
    both = jnp.sum(both.reshape(nzl, nzh, slab, LANES), axis=0)
    both = jnp.sum(lax.all_to_all(both, lines, 0, 0, tiled=True, axis_index_groups=far), axis=0)
    both = lax.all_gather(both, Z, axis=0)
    half = own_ranks // 2
    gram = both[:, slab - half :]
    gram = lax.all_to_all(jnp.broadcast_to(gram[None], (ny, *gram.shape)), "y", 0, 0, tiled=True)
    gram = gram.reshape(2, 2, nzh * nzl, half, LANES).transpose(2, 0, 3, 1, 4).reshape(rank, rank)

    back, orthonormal, squares = finish(gram, left, both, nx)
    squares = lax.psum(lax.psum(squares[:, 0], "core"), "y")
    others = [lax.ppermute(squares, "x", [(i, (i + d) % nx) for i in range(nx)]) for d in range(1, nx)]
    squares = sum(others, squares)
    squares = lax.dynamic_slice_in_dim(squares, lax.axis_index("x") * ranks, ranks, 0)
    back = lax.all_to_all(back, "x", 0, 0, tiled=True)
    new_momentum, mine = join(buffer, back)
    new_basis = (mine / (jnp.sqrt(squares) + column_eps)[:, None]).T
    return (new_momentum, orthonormal, new_basis)


def solution(mesh):
    fine = Mesh(mesh.devices.reshape(4, 4, 4, 4, 2), ("zh", "zl", "x", "y", "core"))
    fsdp, tensor = ("zh", "zl", "x"), ("y", "core")
    return jax.shard_map(
        on_device,
        mesh=fine,
        in_specs=(P(fsdp, tensor), P(fsdp, tensor), P(tensor, fsdp)),
        out_specs=(P(fsdp, tensor), P(fsdp, None), P(tensor, fsdp)),
        check_vma=False,
    )
```
